32 devices in a mesh: grp: 2 (over x), prow: 16 (over z, y, core).
Axes of the slice: x: 2, y: 2, z: 4, core: 2. Of those that a mesh axis runs over, the one named last changes fastest.
Arguments:
- currents: bfloat16 [960, 128, 512], P(('grp', 'prow')), parts along dimension 0, may hold values from -6 to 6
- diag_inverse: bfloat16 [960, 128, 128], P(('grp', 'prow')), parts along dimension 0, as said below
- off_blocks: bfloat16 [960, 2, 128, 128], P(('grp', 'prow')), parts along dimension 0, may hold values from -0.25 to 0.25
- targets: int32 [960, 2], P(('grp', 'prow')), parts along dimension 0, may hold values from -1 to 479, as said below
Outputs:
- solution: bfloat16 [960, 128, 512], P(('grp', 'prow')), parts along dimension 0
The draws below stay inside these ranges and needn't reach their ends.
There are 2 independent parts, one for each index of `grp`. The reference program is written for one: setup_inputs(seed, part) draws one part's arguments, and reference() takes and returns one part's arrays. A program takes and returns all parts, laid end to end along the dimension named above; each array names one. Nothing has to cross between parts.
Inputs may be any that keep to these rules, and one draw needn't show every extreme that they name: targets[n, 0] is -1 exactly for level-3 nodes, else a node of the next level held on the index of prow of n or one beside it; targets[n, 1] is -1 exactly for nodes of levels 2 and 3, else a node two levels up held on the index of prow of n or one beside it. diag_inverse is lower triangular with a positive diagonal.
All inputs are finite; a program needn't handle non-finite values.
Results may differ from the reference program's by a relative error of at most 0.0058.
Values may be sent and summed in bfloat16 or wider, within the bound.
A program may use at most 128 MiB of HBM per device.

```python
import jax
import jax.numpy as jnp
import numpy as np
from jax import lax

SN = 128
R = 512
TOP = 2
NPD = 30
NODES = 480
N_PROW = 16


def draw_diag_inverse(key, part):
    key_numbers, key_diag = jax.random.split(jax.random.fold_in(key, 11))
    rows = lax.broadcasted_iota(jnp.int32, (SN, SN), 0)
    cols = lax.broadcasted_iota(jnp.int32, (SN, SN), 1)
    below = (rows > cols).astype(jnp.float32)
    on_diag = (rows == cols).astype(jnp.float32)
    values = jax.random.normal(key_numbers, (NODES, SN, SN), jnp.float32)
    diagonal_entries = jax.random.uniform(key_diag, (NODES, SN, SN), jnp.float32, 0.8, 1.2)
    result = values * below * SN ** (-0.5) + diagonal_entries * on_diag
    return result.astype(jnp.bfloat16)


def level_start(level):
    return jnp.where(level == 0, 0, jnp.where(level == 1, 8 * TOP, jnp.where(level == 2, 12 * TOP, jnp.where(level == 3, 14 * TOP, 15 * TOP))))


def level_size(level):
    return jnp.where(level == 0, 8 * TOP, jnp.where(level == 1, 4 * TOP, jnp.where(level == 2, 2 * TOP, jnp.where(level == 3, TOP, 1))))


def draw_targets(key, part):
    device_total = NODES // NPD
    node_ids = jnp.arange(NODES, dtype=jnp.int32)
    device_ids = node_ids // NPD
    local_positions = node_ids % NPD
    level = jnp.where(local_positions < 8 * TOP, 0, jnp.where(local_positions < 12 * TOP, 1, jnp.where(local_positions < 14 * TOP, 2, 3)))
    columns = []
    for which in range(2):
        key_dev = jax.random.fold_in(key, 100 + which)
        key_slot = jax.random.fold_in(key, 200 + which)
        step_dev = jax.random.randint(key_dev, (NODES,), -1, 2, jnp.int32)
        owner_partition = jnp.clip(device_ids + step_dev, 0, device_total - 1)
        goal = level + 1 + which
        unmapped_slot = jax.random.randint(key_slot, (NODES,), 0, 1 << 20, jnp.int32)
        slot_ids = unmapped_slot % level_size(goal)
        picked_entries = owner_partition * NPD + level_start(goal) + slot_ids
        columns.append(jnp.where(goal <= 3, picked_entries, -1))
    return jnp.stack(columns, axis=1).astype(jnp.int32)


def level_of(own_key, dims, cuts, low, largest):
    factor_of = 1.0
    for axis_at, shards_of in cuts:
        draws = jax.random.uniform(jax.random.fold_in(jax.random.fold_in(own_key, 6), axis_at), (shards_of,), jnp.float32, low / len(cuts), largest / len(cuts))
        factor_of = factor_of * jnp.repeat(jnp.exp(draws), dims[axis_at] // shards_of).reshape((-1,) + (1,) * (len(dims) - 1 - axis_at))
    return factor_of


def bell_draw(rng, dims, width, bound, cuts=(), held_as=jnp.bfloat16):
    array = width * jax.random.normal(rng, dims, jnp.float32)
    if cuts:
        array = array * level_of(rng, dims, cuts, -0.22, 0.18)
    return jnp.clip(array, -bound, bound).astype(held_as)


def setup_inputs(seed: int = 0, part: int = 0) -> dict:
    key_of = jax.random.split(jax.random.key(seed), 5)
    part_keys = jax.random.split(jax.random.fold_in(key_of[4], part), 5)
    return {
        "currents": bell_draw(part_keys[0], (NODES, SN, R), 1.0, 6.0, ((0, 16),)),
        "diag_inverse": draw_diag_inverse(jax.random.fold_in(jax.random.fold_in(key_of[4], part), 71), part),
        "off_blocks": bell_draw(part_keys[2], (NODES, 2, SN, SN), (4 * SN) ** -0.5, 0.25, ((0, 16),)),
        "targets": draw_targets(jax.random.fold_in(jax.random.fold_in(key_of[4], part), 71), part),
    }


def reference(currents, diag_inverse, off_blocks, targets):
    counts = [8 * TOP, 4 * TOP, 2 * TOP, TOP]
    offsets = [0, 8 * TOP, 12 * TOP, 14 * TOP]
    pending = jnp.zeros((NODES, SN, R), jnp.float32)
    solution = jnp.zeros((NODES, SN, R), jnp.bfloat16)
    for level in range(4):
        node_ids = (np.arange(N_PROW)[:, None] * NPD + offsets[level] + np.arange(counts[level])[None, :]).reshape(-1)
        reduced = (currents[node_ids].astype(jnp.float32) - pending[node_ids]).astype(jnp.bfloat16)
        resolved_unknowns = jnp.einsum("kst,ktr->ksr", diag_inverse[node_ids].astype(jnp.float32), reduced.astype(jnp.float32)).astype(jnp.bfloat16)
        solution = solution.at[node_ids].set(resolved_unknowns)
        if level < 3:
            for which in range(2):
                target_ids = targets[node_ids, which]
                target_ids = jnp.where(target_ids >= 0, target_ids, NODES)
                contrib = jnp.einsum("kst,ktr->ksr", off_blocks[node_ids, which].astype(jnp.float32), resolved_unknowns.astype(jnp.float32))
                pending = pending.at[target_ids].add(contrib, mode="drop")
    return solution
```

```python
import functools

import jax
import jax.numpy as jnp
from jax import lax
from jax.experimental import pallas as pl
from jax.experimental.pallas import tpu as pltpu
from jax.sharding import PartitionSpec as P

MESH = pl.DeviceIdType.MESH
WIDTH = 128


def level_counts(per_device):
    top = per_device // 15
    return [8 * top, 4 * top, 2 * top, top], [0, 8 * top, 12 * top, 14 * top]


def kernel(
    cur, dia, off, tgt, out,
    curv, diav, offv, xs, acc1, acc2, acc3, sb1, sb2, sb3, rb1, rb2, rb3,
    prev1, prev2, prev3, last1, last2, last3,
    in_sem, out_sem, send_sem, recv_sem,
):
    peers = lax.axis_size("prow")
    me = lax.axis_index("prow")
    per_device = cur.shape[0]
    cnt, start = level_counts(per_device)
    chunks = curv.shape[0]
    accs, sbs, rbs = (acc1, acc2, acc3), (sb1, sb2, sb3), (rb1, rb2, rb3)
    prevs, lasts = (prev1, prev2, prev3), (last1, last2, last3)
    has = (me > 0, me < peers - 1)
    n0, n1, n2, n3 = cnt
    senders = start[3]

    def cur_copy(c, group):
        lo, n = ((0, n0), (n0, per_device - n0))[group]
        return pltpu.make_async_copy(
            cur.at[pl.ds(lo, n), :, pl.ds(pl.multiple_of(c * WIDTH, WIDTH), WIDTH)],
            curv.at[c, pl.ds(lo, n)],
            in_sem.at[group, c],
        )

    def weight_copies(group):
        lo, hi = ((0, n0), (n0, per_device))[group]
        hi_off = min(hi, senders)
        return (
            pltpu.make_async_copy(
                dia.at[pl.ds(lo, hi - lo)], diav.at[pl.ds(lo, hi - lo)], in_sem.at[group, chunks]
            ),
            pltpu.make_async_copy(
                off.at[pl.ds(lo, hi_off - lo)], offv.at[pl.ds(lo, hi_off - lo)],
                in_sem.at[group, chunks + 1],
            ),
        )

    def out_copy(level, c):
        lo, n = start[level], cnt[level]
        return pltpu.make_async_copy(
            xs.at[c, pl.ds(lo, n)],
            out.at[pl.ds(lo, n), :, pl.ds(pl.multiple_of(c * WIDTH, WIDTH), WIDTH)],
            out_sem.at[level, c],
        )

    def remote(p, c, d):
        neighbour = jnp.minimum(me + 1, peers - 1) if d else jnp.maximum(me - 1, 0)
        return pltpu.make_async_remote_copy(
            src_ref=sbs[p].at[c, d],
            dst_ref=rbs[p].at[c, 1 - d],
            send_sem=send_sem.at[p, c, d],
            recv_sem=recv_sem.at[p, c, 1 - d],
            device_id={"prow": neighbour},
            device_id_type=MESH,
        )

    for group in range(2):
        first, second = weight_copies(group)
        first.start()
        for c in range(chunks):
            cur_copy(c, group).start()
            if c == 0:
                second.start()

    barrier = pltpu.get_barrier_semaphore()
    for d in range(2):
        @pl.when(has[d])
        def _():
            pl.semaphore_signal(
                barrier, inc=1, device_id={"prow": me + (1 if d else -1)}, device_id_type=MESH
            )

    def column(p, i):
        if p == 0:
            return i, 0
        if p == 1:
            return i, jnp.where(i < n0, 1, 0)
        return n0 + i, jnp.where(i < n1, 1, 0)

    def aim(p, i):
        if isinstance(i, int):
            node, which = (i, 0) if p == 0 else (i, int(i < n0)) if p == 1 else (n0 + i, int(i < n1))
        else:
            node, which = column(p, i)
        return tgt[node, which]

    totals = (n0, n0 + n1, n1 + n2)

    def tables(p):
        total, slots = totals[p], cnt[p + 1]

        @pl.loop(0, total)
        def _(j):
            mine = aim(p, j)
            found = jnp.int32(total)
            for i in range(total):
                found = jnp.where((i < j) & (aim(p, i) == mine), i, found)
            prevs[p][j] = found

        @pl.loop(0, 3 * slots)
        def _(q):
            d = q // slots
            goal = (me + d - 1) * per_device + start[p + 1] + (q - d * slots)
            found = jnp.int32(total)
            for i in range(total):
                found = jnp.where(aim(p, i) == goal, i, found)
            lasts[p][q] = found

    def clear(p):
        @pl.loop(0, chunks)
        def _(c):
            accs[p][c, totals[p]] = jnp.zeros(accs[p].shape[2:], jnp.float32)

    def dot(a, b):
        return jnp.dot(a, b, preferred_element_type=jnp.float32)

    def solve(level, c):
        lo, n = start[level], cnt[level]
        step = min(n, 4)

        @pl.loop(0, n // step)
        def _(b):
            for u in range(step):
                s = b * step + u
                if level == 0:
                    reduced = curv[c, s]
                else:
                    p = level - 1
                    pending = accs[p][c, lasts[p][n + s]] + (
                        rbs[p][c, 0, s].astype(jnp.float32) + rbs[p][c, 1, s].astype(jnp.float32)
                    )
                    reduced = (curv[c, lo + s].astype(jnp.float32) - pending).astype(jnp.bfloat16)
                xs[c, lo + s] = dot(diav[lo + s], reduced).astype(jnp.bfloat16)

    def contribute(level, c):
        lo, n = start[level], cnt[level]
        step = min(n, 4)
        sn = diav.shape[1]

        def add(p, i, value):
            accs[p][c, i] = accs[p][c, prevs[p][i]] + value

        @pl.loop(0, n // step)
        def _(b):
            for u in range(step):
                j = b * step + u
                if level == 2:
                    add(2, n1 + j, dot(offv[lo + j, 0], xs[c, lo + j]))
                else:
                    both = dot(offv[lo + j].reshape(2 * sn, sn), xs[c, lo + j])
                    near, far = (j, j) if level == 0 else (n0 + j, j)
                    add(level, near, both[:sn])
                    add(level + 1, far, both[sn:])

    def send(p, c):
        slots = cnt[p + 1]
        for d in range(2):
            @pl.loop(0, slots)
            def _(s):
                sbs[p][c, d, s] = accs[p][c, lasts[p][2 * d * slots + s]].astype(jnp.bfloat16)

            @pl.when(has[d])
            def _():
                remote(p, c, d).start()

    def receive(p, c):
        for side in range(2):
            @pl.when(has[side])
            def _():
                remote(p, c, 1 - side).wait_recv()

            @pl.when(jnp.logical_not(has[side]))
            def _():
                rbs[p][c, side] = jnp.zeros(rbs[p].shape[2:], jnp.bfloat16)

    tables(0)
    for p in range(3):
        clear(p)
    tables(1)
    first, second = weight_copies(0)
    first.wait()
    second.wait()

    pl.semaphore_wait(barrier, jnp.where(has[0] & has[1], 2, 1))

    @pl.loop(0, chunks)
    def _(c):
        cur_copy(c, 0).wait()
        solve(0, c)
        out_copy(0, c).start()
        contribute(0, c)
        send(0, c)

    tables(2)
    first, second = weight_copies(1)
    first.wait()
    second.wait()

    @pl.loop(0, chunks)
    def _(c):
        cur_copy(c, 1).wait()

    for level in range(1, 4):
        @pl.loop(0, chunks)
        def _(c):
            receive(level - 1, c)
            solve(level, c)
            out_copy(level, c).start()
            if level < 3:
                contribute(level, c)
                send(level, c)

    @pl.loop(0, chunks)
    def _(c):
        for level in range(4):
            out_copy(level, c).wait()
        for p in range(3):
            for d in range(2):
                @pl.when(has[d])
                def _():
                    remote(p, c, d).wait_send()


def on_device(currents, diag_inverse, off_blocks, targets):
    per_device, sn, rhs = currents.shape
    cnt, start = level_counts(per_device)
    n0, n1, n2, n3 = cnt
    chunks = rhs // WIDTH
    totals = (n0, n0 + n1, n1 + n2)
    bf16, f32, i32 = jnp.bfloat16, jnp.float32, jnp.int32
    scratch = [
        pltpu.VMEM((chunks, per_device, sn, WIDTH), bf16),
        pltpu.VMEM((per_device, sn, sn), bf16),
        pltpu.VMEM((start[3], 2, sn, sn), bf16),
        pltpu.VMEM((chunks, per_device, sn, WIDTH), bf16),
    ]
    scratch += [pltpu.VMEM((chunks, t + 1, sn, WIDTH), f32) for t in totals]
    for _ in range(2):
        scratch += [pltpu.VMEM((chunks, 2, n, sn, WIDTH), bf16) for n in cnt[1:]]
    scratch += [pltpu.SMEM((t,), i32) for t in totals]
    scratch += [pltpu.SMEM((3 * n,), i32) for n in cnt[1:]]
    scratch += [
        pltpu.SemaphoreType.DMA((2, chunks + 2)),
        pltpu.SemaphoreType.DMA((4, chunks)),
        pltpu.SemaphoreType.DMA((3, chunks, 2)),
        pltpu.SemaphoreType.DMA((3, chunks, 2)),
    ]
    anywhere = pl.BlockSpec(memory_space=pl.ANY)
    return pl.pallas_call(
        kernel,
        out_shape=jax.ShapeDtypeStruct(currents.shape, currents.dtype),
        in_specs=[anywhere, anywhere, anywhere, pl.BlockSpec(memory_space=pltpu.SMEM)],
        out_specs=anywhere,
        scratch_shapes=scratch,
        compiler_params=pltpu.CompilerParams(
            collective_id=0, has_side_effects=True, vmem_limit_bytes=56 * 1024 * 1024
        ),
    )(currents, diag_inverse, off_blocks, targets)


def solution(mesh):
    placed = (
        P(("grp", "prow"), None, None),
        P(("grp", "prow"), None, None),
        P(("grp", "prow"), None, None, None),
        P(("grp", "prow"), None),
    )
    return jax.shard_map(
        on_device,
        mesh=mesh,
        in_specs=placed,
        out_specs=P(("grp", "prow"), None, None),
        check_vma=False,
    )
```

```python
import functools

import jax
import jax.numpy as jnp
from jax import lax
from jax.experimental import pallas as pl
from jax.experimental.pallas import tpu as pltpu
from jax.sharding import PartitionSpec as P

MESH = pl.DeviceIdType.MESH
WIDTH = 128
PIECES = 3


def level_counts(per_device):
    top = per_device // 15
    return [8 * top, 4 * top, 2 * top, top], [0, 8 * top, 12 * top, 14 * top]


def kernel(
    cur, dia, off, tgt, xs,
    curv, diav, offv, acc1, acc2, acc3, sb1, sb2, sb3, rb1, rb2, rb3,
    prev1, prev2, prev3, last1, last2, last3,
    in_sem, send_sem, recv_sem,
):
    peers = lax.axis_size("prow")
    me = lax.axis_index("prow")
    per_device = cur.shape[0]
    cnt, start = level_counts(per_device)
    chunks = curv.shape[0]
    accs, sbs, rbs = (acc1, acc2, acc3), (sb1, sb2, sb3), (rb1, rb2, rb3)
    prevs, lasts = (prev1, prev2, prev3), (last1, last2, last3)
    has = (me > 0, me < peers - 1)
    n0, n1, n2, n3 = cnt
    senders = start[3]

    def cur_copy(c, group):
        lo, n = ((0, n0), (n0, per_device - n0))[group]
        return pltpu.make_async_copy(
            cur.at[pl.ds(lo, n), :, pl.ds(pl.multiple_of(c * WIDTH, WIDTH), WIDTH)],
            curv.at[c, pl.ds(lo, n)],
            in_sem.at[group, c],
        )

    def weight_copies(group):
        lo, hi = ((0, n0), (n0, per_device))[group]
        hi_off = min(hi, senders)
        return (
            pltpu.make_async_copy(
                dia.at[pl.ds(lo, hi - lo)], diav.at[pl.ds(lo, hi - lo)], in_sem.at[group, chunks]
            ),
            pltpu.make_async_copy(
                off.at[pl.ds(lo, hi_off - lo)], offv.at[pl.ds(lo, hi_off - lo)],
                in_sem.at[group, chunks + 1],
            ),
        )

    def remote(p, c, d):
        neighbour = jnp.minimum(me + 1, peers - 1) if d else jnp.maximum(me - 1, 0)
        return pltpu.make_async_remote_copy(
            src_ref=sbs[p].at[c, d],
            dst_ref=rbs[p].at[c, 1 - d],
            send_sem=send_sem.at[p, c, d],
            recv_sem=recv_sem.at[p, c, 1 - d],
            device_id={"prow": neighbour},
            device_id_type=MESH,
        )

    for group in range(2):
        first, second = weight_copies(group)
        first.start()
        for c in range(chunks):
            cur_copy(c, group).start()
            if c == 0:
                second.start()

    barrier = pltpu.get_barrier_semaphore()
    for d in range(2):
        @pl.when(has[d])
        def _():
            pl.semaphore_signal(
                barrier, inc=1, device_id={"prow": me + (1 if d else -1)}, device_id_type=MESH
            )

    def column(p, i):
        if p == 0:
            return i, 0
        if p == 1:
            return i, jnp.where(i < n0, 1, 0)
        return n0 + i, jnp.where(i < n1, 1, 0)

    def aim(p, i):
        if isinstance(i, int):
            node, which = (i, 0) if p == 0 else (i, int(i < n0)) if p == 1 else (n0 + i, int(i < n1))
        else:
            node, which = column(p, i)
        return tgt[which, node]

    totals = (n0, n0 + n1, n1 + n2)

    def tables(p):
        total, slots = totals[p], cnt[p + 1]

        @pl.loop(0, total)
        def _(j):
            mine = aim(p, j)
            found = jnp.int32(total)
            for i in range(total):
                found = jnp.where((i < j) & (aim(p, i) == mine), i, found)
            prevs[p][j] = found

        @pl.loop(0, 3 * slots)
        def _(q):
            d = q // slots
            goal = (me + d - 1) * per_device + start[p + 1] + (q - d * slots)
            found = jnp.int32(total)
            for i in range(total):
                found = jnp.where(aim(p, i) == goal, i, found)
            lasts[p][q] = found

    def clear(p):
        @pl.loop(0, chunks)
        def _(c):
            accs[p][c, totals[p]] = jnp.zeros(accs[p].shape[2:], jnp.float32)

    def dot(a, b):
        return jnp.dot(a, b, preferred_element_type=jnp.float32)

    def solve(level, c):
        lo, n = start[level], cnt[level]
        step = min(n, 4)

        @pl.loop(0, n // step)
        def _(b):
            for u in range(step):
                s = b * step + u
                if level == 0:
                    reduced = curv[c, s]
                else:
                    p = level - 1
                    pending = accs[p][c, lasts[p][n + s]] + (
                        rbs[p][c, 0, s].astype(jnp.float32) + rbs[p][c, 1, s].astype(jnp.float32)
                    )
                    reduced = (curv[c, lo + s].astype(jnp.float32) - pending).astype(jnp.bfloat16)
                xs[c, lo + s] = dot(diav[lo + s], reduced).astype(jnp.bfloat16)

    def contribute(level, c, which=0):
        lo, n = start[level], cnt[level]
        step = min(n, 4)
        sn = diav.shape[1]

        def add(p, i, value):
            accs[p][c, i] = accs[p][c, prevs[p][i]] + value

        @pl.loop(0, n // step)
        def _(b):
            for u in range(step):
                j = b * step + u
                if level == 0:
                    add(which, j, dot(offv[j, which], xs[c, j]))
                elif level == 2:
                    add(2, n1 + j, dot(offv[lo + j, 0], xs[c, lo + j]))
                else:
                    both = dot(offv[lo + j].reshape(2 * sn, sn), xs[c, lo + j])
                    add(1, n0 + j, both[:sn])
                    add(2, j, both[sn:])

    def send(p, c):
        slots = cnt[p + 1]
        for d in range(2):
            @pl.loop(0, slots)
            def _(s):
                sbs[p][c, d, s] = accs[p][c, lasts[p][2 * d * slots + s]].astype(jnp.bfloat16)

            @pl.when(has[d])
            def _():
                remote(p, c, d).start()

    def receive(p, c):
        for side in range(2):
            @pl.when(has[side])
            def _():
                remote(p, c, 1 - side).wait_recv()

            @pl.when(jnp.logical_not(has[side]))
            def _():
                rbs[p][c, side] = jnp.zeros(rbs[p].shape[2:], jnp.bfloat16)

    tables(0)
    clear(0)
    first, second = weight_copies(0)
    first.wait()
    second.wait()

    pl.semaphore_wait(barrier, jnp.where(has[0] & has[1], 2, 1))

    @pl.loop(0, chunks)
    def _(c):
        cur_copy(c, 0).wait()
        solve(0, c)
        contribute(0, c)
        send(0, c)

    clear(1)
    clear(2)
    tables(1)
    tables(2)

    @pl.loop(0, chunks)
    def _(c):
        contribute(0, c, 1)

    first, second = weight_copies(1)
    first.wait()
    second.wait()

    @pl.loop(0, chunks)
    def _(c):
        cur_copy(c, 1).wait()

    for level in range(1, 4):
        @pl.loop(0, chunks)
        def _(c):
            receive(level - 1, c)
            solve(level, c)
            if level < 3:
                contribute(level, c)
                send(level, c)

    @pl.loop(0, chunks)
    def _(c):
        for p in range(3):
            for d in range(2):
                @pl.when(has[d])
                def _():
                    remote(p, c, d).wait_send()


def write_out(solved, out, sem):
    chunks, nodes = solved.shape[0], solved.shape[1]
    part = nodes // PIECES
    copies = [
        pltpu.make_async_copy(
            solved.at[c, pl.ds(k * part, part)],
            out.at[pl.ds(k * part, part), :, pl.ds(c * WIDTH, WIDTH)],
            sem.at[c, k],
        )
        for c in range(chunks)
        for k in range(PIECES)
    ]
    for copy in copies:
        copy.start()
    for copy in copies:
        copy.wait()


def on_device(currents, diag_inverse, off_blocks, targets):
    per_device, sn, rhs = currents.shape
    cnt, start = level_counts(per_device)
    n0, n1, n2, n3 = cnt
    chunks = rhs // WIDTH
    totals = (n0, n0 + n1, n1 + n2)
    bf16, f32, i32 = jnp.bfloat16, jnp.float32, jnp.int32
    scratch = [
        pltpu.VMEM((chunks, per_device, sn, WIDTH), bf16),
        pltpu.VMEM((per_device, sn, sn), bf16),
        pltpu.VMEM((start[3], 2, sn, sn), bf16),
    ]
    scratch += [pltpu.VMEM((chunks, t + 1, sn, WIDTH), f32) for t in totals]
    for _ in range(2):
        scratch += [pltpu.VMEM((chunks, 2, n, sn, WIDTH), bf16) for n in cnt[1:]]
    scratch += [pltpu.SMEM((t,), i32) for t in totals]
    scratch += [pltpu.SMEM((3 * n,), i32) for n in cnt[1:]]
    scratch += [
        pltpu.SemaphoreType.DMA((2, chunks + 2)),
        pltpu.SemaphoreType.DMA((3, chunks, 2)),
        pltpu.SemaphoreType.DMA((3, chunks, 2)),
    ]
    anywhere = pl.BlockSpec(memory_space=pl.ANY)
    solved = pl.pallas_call(
        kernel,
        out_shape=pltpu.VMEM((chunks, per_device, sn, WIDTH), bf16),
        in_specs=[anywhere, anywhere, anywhere, pl.BlockSpec(memory_space=pltpu.SMEM)],
        out_specs=pl.BlockSpec(memory_space=pltpu.VMEM),
        scratch_shapes=scratch,
        compiler_params=pltpu.CompilerParams(
            collective_id=0, has_side_effects=True, vmem_limit_bytes=56 * 1024 * 1024
        ),
    )(currents, diag_inverse, off_blocks, targets.T)
    return pl.pallas_call(
        write_out,
        out_shape=jax.ShapeDtypeStruct(currents.shape, currents.dtype),
        in_specs=[anywhere],
        out_specs=anywhere,
        scratch_shapes=[pltpu.SemaphoreType.DMA((chunks, PIECES))],
        compiler_params=pltpu.CompilerParams(vmem_limit_bytes=2 * 1024 * 1024),
    )(pltpu.with_memory_space_constraint(solved, pltpu.VMEM))


def solution(mesh):
    placed = (
        P(("grp", "prow"), None, None),
        P(("grp", "prow"), None, None),
        P(("grp", "prow"), None, None, None),
        P(("grp", "prow"), None),
    )
    return jax.shard_map(
        on_device,
        mesh=mesh,
        in_specs=placed,
        out_specs=P(("grp", "prow"), None, None),
        check_vma=False,
    )
```

```python
import functools

import jax
import jax.numpy as jnp
from jax import lax
from jax.experimental import pallas as pl
from jax.experimental.pallas import tpu as pltpu
from jax.sharding import PartitionSpec as P

MESH = pl.DeviceIdType.MESH
WIDTH = 128
PIECES = 6


def level_counts(per_device):
    top = per_device // 15
    return [8 * top, 4 * top, 2 * top, top], [0, 8 * top, 12 * top, 14 * top]


def kernel(
    cur, dia, off, tgt, xs,
    curv, diav, offv, acc1, acc2, acc3, sb1, sb2, sb3, rb1, rb2, rb3,
    prev1, prev2, prev3, last1, last2, last3,
    in_sem, send_sem, recv_sem,
):
    peers = lax.axis_size("prow")
    me = lax.axis_index("prow")
    per_device = cur.shape[0]
    cnt, start = level_counts(per_device)
    chunks = curv.shape[0]
    accs, sbs, rbs = (acc1, acc2, acc3), (sb1, sb2, sb3), (rb1, rb2, rb3)
    prevs, lasts = (prev1, prev2, prev3), (last1, last2, last3)
    has = (me > 0, me < peers - 1)
    n0, n1, n2, n3 = cnt
    senders = start[3]

    def cur_copy(c, group):
        lo, n = ((0, n0), (n0, per_device - n0))[group]
        return pltpu.make_async_copy(
            cur.at[pl.ds(lo, n), :, pl.ds(pl.multiple_of(c * WIDTH, WIDTH), WIDTH)],
            curv.at[c, pl.ds(lo, n)],
            in_sem.at[group, c],
        )

    def weight_copies(group):
        lo, hi = ((0, n0), (n0, per_device))[group]
        hi_off = min(hi, senders)
        return (
            pltpu.make_async_copy(
                dia.at[pl.ds(lo, hi - lo)], diav.at[pl.ds(lo, hi - lo)], in_sem.at[group, chunks]
            ),
            pltpu.make_async_copy(
                off.at[pl.ds(lo, hi_off - lo)], offv.at[pl.ds(lo, hi_off - lo)],
                in_sem.at[group, chunks + 1],
            ),
        )

    def remote(p, c, d):
        neighbour = jnp.minimum(me + 1, peers - 1) if d else jnp.maximum(me - 1, 0)
        return pltpu.make_async_remote_copy(
            src_ref=sbs[p].at[c, d],
            dst_ref=rbs[p].at[c, 1 - d],
            send_sem=send_sem.at[p, c, d],
            recv_sem=recv_sem.at[p, c, 1 - d],
            device_id={"prow": neighbour},
            device_id_type=MESH,
        )

    def load(group):
        first, second = weight_copies(group)
        first.start()
        for c in range(chunks):
            cur_copy(c, group).start()
            if c == 0:
                second.start()

    load(0)

    barrier = pltpu.get_barrier_semaphore()
    for d in range(2):
        @pl.when(has[d])
        def _():
            pl.semaphore_signal(
                barrier, inc=1, device_id={"prow": me + (1 if d else -1)}, device_id_type=MESH
            )

    def column(p, i):
        if p == 0:
            return i, 0
        if p == 1:
            return i, jnp.where(i < n0, 1, 0)
        return n0 + i, jnp.where(i < n1, 1, 0)

    def aim(p, i):
        if isinstance(i, int):
            node, which = (i, 0) if p == 0 else (i, int(i < n0)) if p == 1 else (n0 + i, int(i < n1))
        else:
            node, which = column(p, i)
        return tgt[which, node]

    totals = (n0, n0 + n1, n1 + n2)

    def tables(p):
        total, slots = totals[p], cnt[p + 1]

        @pl.loop(0, total)
        def _(j):
            mine = aim(p, j)
            found = jnp.int32(total)
            for i in range(total):
                found = jnp.where((i < j) & (aim(p, i) == mine), i, found)
            prevs[p][j] = found

        chain_ends(p, 0)
        chain_ends(p, 2)

    def chain_ends(p, d):
        total, slots = totals[p], cnt[p + 1]

        @pl.loop(d * slots, (d + 1) * slots)
        def _(q):
            goal = (me + d - 1) * per_device + start[p + 1] + (q - d * slots)
            found = jnp.int32(total)
            for i in range(total):
                found = jnp.where(aim(p, i) == goal, i, found)
            lasts[p][q] = found

    def clear(p):
        @pl.loop(0, chunks)
        def _(c):
            accs[p][c, totals[p]] = jnp.zeros(accs[p].shape[2:], jnp.float32)

    def columns(c):
        return pl.ds(pl.multiple_of(c * WIDTH, WIDTH), WIDTH)

    def dot(a, b):
        return jnp.dot(a, b, preferred_element_type=jnp.float32)

    def solve(level, c):
        lo, n = start[level], cnt[level]
        step = min(n, 4)

        @pl.loop(0, n // step)
        def _(b):
            for u in range(step):
                s = b * step + u
                if level == 0:
                    reduced = curv[c, s]
                else:
                    p = level - 1
                    pending = accs[p][c, lasts[p][n + s]] + (
                        rbs[p][c, 0, s].astype(jnp.float32) + rbs[p][c, 1, s].astype(jnp.float32)
                    )
                    reduced = (curv[c, lo + s].astype(jnp.float32) - pending).astype(jnp.bfloat16)
                xs[lo + s, :, columns(c)] = dot(diav[lo + s], reduced).astype(jnp.bfloat16)

    def contribute(level, c, which=0):
        lo, n = start[level], cnt[level]
        step = min(n, 4)
        sn = diav.shape[1]

        def add(p, i, value):
            accs[p][c, i] = accs[p][c, prevs[p][i]] + value

        @pl.loop(0, n // step)
        def _(b):
            for u in range(step):
                j = b * step + u
                if level == 0:
                    add(which, j, dot(offv[j, which], xs[j, :, columns(c)]))
                elif level == 2:
                    add(2, n1 + j, dot(offv[lo + j, 0], xs[lo + j, :, columns(c)]))
                else:
                    both = dot(offv[lo + j].reshape(2 * sn, sn), xs[lo + j, :, columns(c)])
                    add(1, n0 + j, both[:sn])
                    add(2, j, both[sn:])

    def send(p, c):
        slots = cnt[p + 1]
        for k in range(2):
            right = lax.rem(me + k, 2)

            @pl.loop(0, slots)
            def _(s):
                sbs[p][c, right, s] = accs[p][c, lasts[p][2 * right * slots + s]].astype(
                    jnp.bfloat16
                )

            for d in range(2):
                @pl.when(has[d] & (right == d))
                def _():
                    remote(p, c, d).start()

    def receive(p, c):
        for side in range(2):
            @pl.when(has[side])
            def _():
                remote(p, c, 1 - side).wait_recv()

            @pl.when(jnp.logical_not(has[side]))
            def _():
                rbs[p][c, side] = jnp.zeros(rbs[p].shape[2:], jnp.bfloat16)

    tables(0)
    load(1)
    clear(0)
    first, second = weight_copies(0)
    first.wait()
    second.wait()

    pl.semaphore_wait(barrier, jnp.where(has[0] & has[1], 2, 1))

    @pl.loop(0, chunks)
    def _(c):
        cur_copy(c, 0).wait()
        solve(0, c)
        contribute(0, c)
        send(0, c)

    clear(1)
    clear(2)
    tables(1)
    tables(2)
    for p in range(3):
        chain_ends(p, 1)

    @pl.loop(0, chunks)
    def _(c):
        contribute(0, c, 1)

    first, second = weight_copies(1)
    first.wait()
    second.wait()

    @pl.loop(0, chunks)
    def _(c):
        cur_copy(c, 1).wait()

    for level in range(1, 4):
        @pl.loop(0, chunks)
        def _(c):
            receive(level - 1, c)
            solve(level, c)
            if level < 3:
                contribute(level, c)
                send(level, c)

    @pl.loop(0, chunks)
    def _(c):
        for p in range(3):
            for d in range(2):
                @pl.when(has[d])
                def _():
                    remote(p, c, d).wait_send()


def write_out(solved, out, sem):
    part = solved.shape[0] // PIECES
    copies = [
        pltpu.make_async_copy(
            solved.at[pl.ds(k * part, part)], out.at[pl.ds(k * part, part)], sem.at[k]
        )
        for k in range(PIECES)
    ]
    for copy in copies:
        copy.start()
    for copy in copies:
        copy.wait()


def on_device(currents, diag_inverse, off_blocks, targets):
    per_device, sn, rhs = currents.shape
    cnt, start = level_counts(per_device)
    n0, n1, n2, n3 = cnt
    chunks = rhs // WIDTH
    totals = (n0, n0 + n1, n1 + n2)
    bf16, f32, i32 = jnp.bfloat16, jnp.float32, jnp.int32
    scratch = [
        pltpu.VMEM((chunks, per_device, sn, WIDTH), bf16),
        pltpu.VMEM((per_device, sn, sn), bf16),
        pltpu.VMEM((start[3], 2, sn, sn), bf16),
    ]
    scratch += [pltpu.VMEM((chunks, t + 1, sn, WIDTH), f32) for t in totals]
    for _ in range(2):
        scratch += [pltpu.VMEM((chunks, 2, n, sn, WIDTH), bf16) for n in cnt[1:]]
    scratch += [pltpu.SMEM((t,), i32) for t in totals]
    scratch += [pltpu.SMEM((3 * n,), i32) for n in cnt[1:]]
    scratch += [
        pltpu.SemaphoreType.DMA((2, chunks + 2)),
        pltpu.SemaphoreType.DMA((3, chunks, 2)),
        pltpu.SemaphoreType.DMA((3, chunks, 2)),
    ]
    anywhere = pl.BlockSpec(memory_space=pl.ANY)
    solved = pl.pallas_call(
        kernel,
        out_shape=pltpu.VMEM(currents.shape, bf16),
        in_specs=[anywhere, anywhere, anywhere, pl.BlockSpec(memory_space=pltpu.SMEM)],
        out_specs=pl.BlockSpec(memory_space=pltpu.VMEM),
        scratch_shapes=scratch,
        compiler_params=pltpu.CompilerParams(
            collective_id=0, has_side_effects=True, vmem_limit_bytes=56 * 1024 * 1024
        ),
    )(currents, diag_inverse, off_blocks, targets.T)
    return pl.pallas_call(
        write_out,
        out_shape=jax.ShapeDtypeStruct(currents.shape, currents.dtype),
        in_specs=[anywhere],
        out_specs=anywhere,
        scratch_shapes=[pltpu.SemaphoreType.DMA((PIECES,))],
        compiler_params=pltpu.CompilerParams(vmem_limit_bytes=2 * 1024 * 1024),
    )(pltpu.with_memory_space_constraint(solved, pltpu.VMEM))


def solution(mesh):
    placed = (
        P(("grp", "prow"), None, None),
        P(("grp", "prow"), None, None),
        P(("grp", "prow"), None, None, None),
        P(("grp", "prow"), None),
    )
    return jax.shard_map(
        on_device,
        mesh=mesh,
        in_specs=placed,
        out_specs=P(("grp", "prow"), None, None),
        check_vma=False,
    )
```

```python
import functools

import jax
import jax.numpy as jnp
from jax import lax
from jax.experimental import pallas as pl
from jax.experimental.pallas import tpu as pltpu
from jax.sharding import PartitionSpec as P

MESH = pl.DeviceIdType.MESH
WIDTH = 128
PIECES = 6


def level_counts(per_device):
    top = per_device // 15
    return [8 * top, 4 * top, 2 * top, top], [0, 8 * top, 12 * top, 14 * top]


def kernel(
    cur, dia, off, tgt, xs,
    curv, diav, offv, acc1, acc2, acc3, sb1, sb2, sb3, rb1, rb2, rb3,
    prev1, prev2, prev3, last1, last2, last3,
    in_sem, send_sem, recv_sem,
):
    peers = lax.axis_size("prow")
    me = lax.axis_index("prow")
    per_device = cur.shape[0]
    cnt, start = level_counts(per_device)
    chunks = curv.shape[0]
    accs, sbs, rbs = (acc1, acc2, acc3), (sb1, sb2, sb3), (rb1, rb2, rb3)
    prevs, lasts = (prev1, prev2, prev3), (last1, last2, last3)
    has = (me > 0, me < peers - 1)
    n0, n1, n2, n3 = cnt
    senders = start[3]

    def cur_copy(c, group):
        lo, n = ((0, n0), (n0, per_device - n0))[group]
        return pltpu.make_async_copy(
            cur.at[pl.ds(lo, n), :, pl.ds(pl.multiple_of(c * WIDTH, WIDTH), WIDTH)],
            curv.at[c, pl.ds(lo, n)],
            in_sem.at[group, c],
        )

    def weight_copies(group):
        lo, hi = ((0, n0), (n0, per_device))[group]
        hi_off = min(hi, senders)
        return (
            pltpu.make_async_copy(
                dia.at[pl.ds(lo, hi - lo)], diav.at[pl.ds(lo, hi - lo)], in_sem.at[group, chunks]
            ),
            pltpu.make_async_copy(
                off.at[pl.ds(lo, hi_off - lo)], offv.at[pl.ds(lo, hi_off - lo)],
                in_sem.at[group, chunks + 1],
            ),
        )

    def remote(p, c, d):
        neighbour = jnp.minimum(me + 1, peers - 1) if d else jnp.maximum(me - 1, 0)
        return pltpu.make_async_remote_copy(
            src_ref=sbs[p].at[c, d],
            dst_ref=rbs[p].at[c, 1 - d],
            send_sem=send_sem.at[p, c, d],
            recv_sem=recv_sem.at[p, c, 1 - d],
            device_id={"prow": neighbour},
            device_id_type=MESH,
        )

    def load(group):
        first, second = weight_copies(group)
        first.start()
        for c in range(chunks):
            cur_copy(c, group).start()
            if c == 0:
                second.start()

    load(0)

    barrier = pltpu.get_barrier_semaphore()
    for d in range(2):
        @pl.when(has[d])
        def _():
            pl.semaphore_signal(
                barrier, inc=1, device_id={"prow": me + (1 if d else -1)}, device_id_type=MESH
            )

    def column(p, i):
        if p == 0:
            return i, 0
        if p == 1:
            return i, jnp.where(i < n0, 1, 0)
        return n0 + i, jnp.where(i < n1, 1, 0)

    def aim(p, i):
        if isinstance(i, int):
            node, which = (i, 0) if p == 0 else (i, int(i < n0)) if p == 1 else (n0 + i, int(i < n1))
        else:
            node, which = column(p, i)
        return tgt[which, node]

    totals = (n0, n0 + n1, n1 + n2)

    def tables(p):
        total, slots = totals[p], cnt[p + 1]

        @pl.loop(0, total)
        def _(j):
            mine = aim(p, j)
            found = jnp.int32(total)
            for i in range(total):
                found = jnp.where((i < j) & (aim(p, i) == mine), i, found)
            prevs[p][j] = found

        chain_ends(p, 0)
        chain_ends(p, 2)

    def chain_ends(p, d):
        total, slots = totals[p], cnt[p + 1]

        @pl.loop(d * slots, (d + 1) * slots)
        def _(q):
            goal = (me + d - 1) * per_device + start[p + 1] + (q - d * slots)
            found = jnp.int32(total)
            for i in range(total):
                found = jnp.where(aim(p, i) == goal, i, found)
            lasts[p][q] = found

    def clear(p):
        @pl.loop(0, chunks)
        def _(c):
            accs[p][c, totals[p]] = jnp.zeros(accs[p].shape[2:], jnp.float32)

    def columns(c):
        return pl.ds(pl.multiple_of(c * WIDTH, WIDTH), WIDTH)

    def dot(a, b):
        return jnp.dot(a, b, preferred_element_type=jnp.float32)

    def solve(level, c):
        lo, n = start[level], cnt[level]
        step = min(n, 8)

        @pl.loop(0, n // step)
        def _(b):
            for u in range(step):
                s = b * step + u
                if level == 0:
                    reduced = curv[c, s]
                else:
                    p = level - 1
                    pending = accs[p][c, lasts[p][n + s]] + (
                        rbs[p][c, 0, s].astype(jnp.float32) + rbs[p][c, 1, s].astype(jnp.float32)
                    )
                    reduced = (curv[c, lo + s].astype(jnp.float32) - pending).astype(jnp.bfloat16)
                xs[lo + s, :, columns(c)] = dot(diav[lo + s], reduced).astype(jnp.bfloat16)

    def contribute(level, c, which=0):
        lo, n = start[level], cnt[level]
        step = min(n, 8)
        sn = diav.shape[1]

        def add(p, i, value):
            accs[p][c, i] = accs[p][c, prevs[p][i]] + value

        @pl.loop(0, n // step)
        def _(b):
            for u in range(step):
                j = b * step + u
                if level == 0:
                    add(which, j, dot(offv[j, which], xs[j, :, columns(c)]))
                elif level == 2:
                    add(2, n1 + j, dot(offv[lo + j, 0], xs[lo + j, :, columns(c)]))
                else:
                    both = dot(offv[lo + j].reshape(2 * sn, sn), xs[lo + j, :, columns(c)])
                    add(1, n0 + j, both[:sn])
                    add(2, j, both[sn:])

    def send(p, c):
        slots = cnt[p + 1]
        for k in range(2):
            right = lax.rem(me + k, 2)

            @pl.loop(0, slots)
            def _(s):
                sbs[p][c, right, s] = accs[p][c, lasts[p][2 * right * slots + s]].astype(
                    jnp.bfloat16
                )

            for d in range(2):
                @pl.when(has[d] & (right == d))
                def _():
                    remote(p, c, d).start()

    def receive(p, c):
        for side in range(2):
            @pl.when(has[side])
            def _():
                remote(p, c, 1 - side).wait_recv()

            @pl.when(jnp.logical_not(has[side]))
            def _():
                rbs[p][c, side] = jnp.zeros(rbs[p].shape[2:], jnp.bfloat16)

    tables(0)
    load(1)
    clear(0)
    first, second = weight_copies(0)
    first.wait()
    second.wait()

    pl.semaphore_wait(barrier, jnp.where(has[0] & has[1], 2, 1))

    @pl.loop(0, chunks)
    def _(c):
        cur_copy(c, 0).wait()
        solve(0, c)
        contribute(0, c)
        send(0, c)

    clear(1)
    clear(2)
    tables(1)
    tables(2)
    for p in range(3):
        chain_ends(p, 1)

    @pl.loop(0, chunks)
    def _(c):
        contribute(0, c, 1)

    first, second = weight_copies(1)
    first.wait()
    second.wait()

    @pl.loop(0, chunks)
    def _(c):
        cur_copy(c, 1).wait()

    for level in range(1, 4):
        @pl.loop(0, chunks)
        def _(c):
            receive(level - 1, c)
            solve(level, c)
            if level < 3:
                contribute(level, c)
                send(level, c)

    @pl.loop(0, chunks)
    def _(c):
        for p in range(3):
            for d in range(2):
                @pl.when(has[d])
                def _():
                    remote(p, c, d).wait_send()


def write_out(solved, out, sem):
    part = solved.shape[0] // PIECES
    copies = [
        pltpu.make_async_copy(
            solved.at[pl.ds(k * part, part)], out.at[pl.ds(k * part, part)], sem.at[k]
        )
        for k in range(PIECES)
    ]
    for copy in copies:
        copy.start()
    for copy in copies:
        copy.wait()


def on_device(currents, diag_inverse, off_blocks, targets):
    per_device, sn, rhs = currents.shape
    cnt, start = level_counts(per_device)
    n0, n1, n2, n3 = cnt
    chunks = rhs // WIDTH
    totals = (n0, n0 + n1, n1 + n2)
    bf16, f32, i32 = jnp.bfloat16, jnp.float32, jnp.int32
    scratch = [
        pltpu.VMEM((chunks, per_device, sn, WIDTH), bf16),
        pltpu.VMEM((per_device, sn, sn), bf16),
        pltpu.VMEM((start[3], 2, sn, sn), bf16),
    ]
    scratch += [pltpu.VMEM((chunks, t + 1, sn, WIDTH), f32) for t in totals]
    for _ in range(2):
        scratch += [pltpu.VMEM((chunks, 2, n, sn, WIDTH), bf16) for n in cnt[1:]]
    scratch += [pltpu.SMEM((t,), i32) for t in totals]
    scratch += [pltpu.SMEM((3 * n,), i32) for n in cnt[1:]]
    scratch += [
        pltpu.SemaphoreType.DMA((2, chunks + 2)),
        pltpu.SemaphoreType.DMA((3, chunks, 2)),
        pltpu.SemaphoreType.DMA((3, chunks, 2)),
    ]
    anywhere = pl.BlockSpec(memory_space=pl.ANY)
    solved = pl.pallas_call(
        kernel,
        out_shape=pltpu.VMEM(currents.shape, bf16),
        in_specs=[anywhere, anywhere, anywhere, pl.BlockSpec(memory_space=pltpu.SMEM)],
        out_specs=pl.BlockSpec(memory_space=pltpu.VMEM),
        scratch_shapes=scratch,
        compiler_params=pltpu.CompilerParams(
            collective_id=0, has_side_effects=True, vmem_limit_bytes=56 * 1024 * 1024
        ),
    )(currents, diag_inverse, off_blocks, targets.T)
    return pl.pallas_call(
        write_out,
        out_shape=jax.ShapeDtypeStruct(currents.shape, currents.dtype),
        in_specs=[anywhere],
        out_specs=anywhere,
        scratch_shapes=[pltpu.SemaphoreType.DMA((PIECES,))],
        compiler_params=pltpu.CompilerParams(vmem_limit_bytes=2 * 1024 * 1024),
    )(pltpu.with_memory_space_constraint(solved, pltpu.VMEM))


def solution(mesh):
    placed = (
        P(("grp", "prow"), None, None),
        P(("grp", "prow"), None, None),
        P(("grp", "prow"), None, None, None),
        P(("grp", "prow"), None),
    )
    return jax.shard_map(
        on_device,
        mesh=mesh,
        in_specs=placed,
        out_specs=P(("grp", "prow"), None, None),
        check_vma=False,
    )
```
